512 devices in a mesh: rng: 64 (over y_lo, x, z), chan: 8 (over y_hi, core).
Axes of the slice: x: 4, y: 8 (y_hi: 4, y_lo: 2; y = y_hi * 2 + y_lo), z: 8, core: 2. Of those that a mesh axis runs over, the one named last changes fastest.
Arguments:
- samples: bfloat16 [2, 4, 512, 32768], P(None, None, 'chan', 'rng'), may hold values from -6 to 6
- phase_codes: int32 [16, 128], replicated, may hold values from 0 to 15
- block_pattern: int32 [16, 8], replicated, may hold values 0 or 1
- steering: bfloat16 [2, 8, 64], replicated, may hold values from -0.75 to 0.75
Outputs:
- normalized: float32 [8, 512, 32768], P('chan', 'rng')
The draws below stay inside these ranges and needn't reach their ends.
All inputs are finite; a program needn't handle non-finite values.
Results may differ from the reference program's by a relative error of at most 0.015.
Values may be sent and summed in bfloat16 or wider, within the bound.
A program may use at most 64 MiB of HBM per device.

```python
import math
import jax
import jax.numpy as jnp
from jax import lax

TX = 16
RX = 4
CHIPS = 128
BLOCKS = 8
PHASES = 16
PULSES = 512
BEAMS = 8
GATES = 32768


def plant(values, stream_key, least, top_value):
    longest = values.shape.index(max(values.shape))
    spots = []
    for shift in (0, 1):
        where = [jax.random.randint(jax.random.fold_in(stream_key, axis), (), 0, length) for axis, length in enumerate(values.shape)]
        where[longest] = (where[longest] + shift) % values.shape[longest]
        spots.append(tuple(where))
    return values.at[spots[0]].set(least).at[spots[1]].set(top_value)


def block_scale(stream_key, extent, split, smallest, largest):
    gain, own = 1.0, jax.random.fold_in(stream_key, 6)
    for axis_at, shards_of in split:
        heights = jnp.exp(jax.random.uniform(jax.random.fold_in(own, axis_at), (shards_of,), jnp.float32, smallest / len(split), largest / len(split)))
        gain = gain * jnp.repeat(heights, extent[axis_at] // shards_of).reshape([-1 if axis == axis_at else 1 for axis in range(len(extent))])
    return gain


def scatter_about(stream_key, shape, scale, limit, pieces=(), kind=jnp.bfloat16):
    result = scale * jax.random.normal(stream_key, shape, jnp.float32)
    if pieces:
        result = result * block_scale(stream_key, shape, pieces, -0.22, 0.18)
    return jnp.clip(result, -limit, limit).astype(kind)


def setup_inputs(seed: int = 0) -> dict:
    streams_of = jax.random.split(jax.random.key(seed), 5)
    return {
        "samples": scatter_about(streams_of[0], (2, RX, PULSES, GATES), 1.0, 6.0, ((2, 8), (3, 64))),
        "phase_codes": plant(jax.random.randint(streams_of[1], (TX, CHIPS), 0, PHASES), jax.random.fold_in(streams_of[1], 1), 0, PHASES - 1).astype(jnp.int32),
        "block_pattern": plant((jax.random.randint(streams_of[2], (TX, BLOCKS), 0, 4) < 3).astype(jnp.int32), jax.random.fold_in(streams_of[2], 1), 0, 1),
        "steering": scatter_about(streams_of[3], (2, BEAMS, TX * RX), (TX * RX) ** -0.5, 0.75),
    }


def keep_rounded(values):
    return lax.optimization_barrier(values.astype(jnp.bfloat16)).astype(jnp.float32)


def reference(samples, phase_codes, block_pattern, steering):
    length = 2 * GATES
    per_block = CHIPS // BLOCKS
    active = jnp.repeat(block_pattern.astype(jnp.float32), per_block, axis=1)
    code_phase = phase_codes.astype(jnp.float32) * (2.0 * math.pi / PHASES)
    code_re = keep_rounded(jnp.cos(code_phase) * active)
    code_im = keep_rounded(jnp.sin(code_phase) * active)
    code_spec = jnp.conj(jnp.fft.fft(lax.complex(code_re, code_im), n=length, axis=1))
    data = samples.astype(jnp.float32)
    data_spec = jnp.fft.fft(lax.complex(data[0], data[1]), n=length, axis=2)
    weights = steering.astype(jnp.float32)

    def add_pair(total, pair):
        receiver = pair // TX
        sender = pair % TX
        correlated = jnp.fft.ifft(data_spec[receiver] * code_spec[sender][None, :], axis=1)[:, :GATES]
        match_re = keep_rounded(jnp.real(correlated))
        match_im = keep_rounded(jnp.imag(correlated))
        weight_re = weights[0, :, pair][:, None, None]
        weight_im = weights[1, :, pair][:, None, None]
        beam_re = weight_re * match_re[None] - weight_im * match_im[None]
        beam_im = weight_im * match_re[None] + weight_re * match_im[None]
        return total + jnp.stack([beam_re, beam_im]), None

    start = jnp.zeros((2, BEAMS, PULSES, GATES), jnp.float32)
    total, _ = lax.scan(add_pair, start, jnp.arange(TX * RX, dtype=jnp.int32))
    beams = keep_rounded(total)
    spectrum = jnp.fft.fft(lax.complex(beams[0], beams[1]), axis=1)
    spec_re = keep_rounded(jnp.real(spectrum))
    spec_im = keep_rounded(jnp.imag(spectrum))
    power = keep_rounded(spec_re * spec_re + spec_im * spec_im)
    average = jnp.mean(power, axis=2, keepdims=True)
    return power / (average + 1e-6)
```

```python
import functools
import math

import jax
import jax.numpy as jnp
import numpy as np
from jax import lax
from jax.experimental import pallas as pl
from jax.experimental.pallas import tpu as pltpu
from jax.sharding import PartitionSpec as P

PHASES = 16
LANES = 128
MESH = pl.DeviceIdType.MESH


def dft_table(pulse_count):
    index = np.arange(pulse_count)
    angles = (np.outer(index, index) % pulse_count) * (2.0 * math.pi / pulse_count)
    cosine, sine = np.cos(angles), np.sin(angles)
    table = np.concatenate(
        [np.concatenate([cosine, sine], axis=1), np.concatenate([-sine, cosine], axis=1)]
    )
    return jnp.asarray(table, jnp.bfloat16)


def dot(left, right):
    return jnp.dot(left, right, preferred_element_type=jnp.float32)


def kernel(
    rng_count,
    chan_count,
    samples_ref,
    codes_ref,
    pattern_ref,
    steering_ref,
    table_hbm,
    out_ref,
    extended,
    table,
    taps,
    filters,
    lines,
    outgoing,
    gathered,
    power_out,
    power_in,
    load_sem,
    table_sem,
    edge_sem,
    beam_send,
    beam_recv,
    power_send,
    power_recv,
):
    rng = lax.axis_index("rng")
    chan = lax.axis_index("chan")
    rx_count, pulses, gates = samples_ref.shape[1:]
    chips = codes_ref.shape[1]
    chunks = outgoing.shape[0]
    width = outgoing.shape[4]
    per_chunk = width // LANES
    bins = table.shape[0] // 2
    own_bins = bins // rng_count

    load = pltpu.make_async_copy(samples_ref, extended.at[:, :, :, pl.ds(0, gates)], load_sem)
    load.start()
    table_load = pltpu.make_async_copy(table_hbm, table, table_sem)
    table_load.start()

    barrier = pltpu.get_barrier_semaphore()

    @pl.loop(1, chan_count)
    def _(step):
        peer = lax.rem(chan + step, chan_count)
        pl.semaphore_signal(barrier, inc=1, device_id={"chan": peer}, device_id_type=MESH)

    @pl.loop(1, rng_count)
    def _(step):
        peer = lax.rem(rng + step, rng_count)
        pl.semaphore_signal(barrier, inc=1, device_id={"rng": peer}, device_id_type=MESH)

    tx_count, block_count = pattern_ref.shape
    spread = (
        lax.broadcasted_iota(jnp.int32, (block_count, chips), 1) // (chips // block_count)
        == lax.broadcasted_iota(jnp.int32, (block_count, chips), 0)
    ).astype(jnp.float32)
    active = dot(pattern_ref[...].astype(jnp.float32), spread)
    phase = codes_ref[...].astype(jnp.float32) * (2.0 * math.pi / PHASES)
    code_re = (jnp.cos(phase) * active).astype(jnp.bfloat16)
    code_im = (jnp.sin(phase) * active).astype(jnp.bfloat16)
    reverse = (
        lax.rem(
            lax.broadcasted_iota(jnp.int32, (chips, 2 * chips), 0)
            + lax.broadcasted_iota(jnp.int32, (chips, 2 * chips), 1),
            2 * chips,
        )
        == 0
    ).astype(jnp.bfloat16)
    back_re = dot(code_re, reverse)
    back_im = dot(code_im, reverse)
    weights = steering_ref[...]
    beam_count = weights.shape[0] // 2
    row = lax.broadcasted_iota(jnp.int32, (rx_count * tx_count, 2 * chips), 0) // tx_count
    for rx in range(rx_count):
        wide_re = jnp.where(row == rx, jnp.concatenate([back_re] * rx_count, 0), 0.0)
        wide_im = jnp.where(row == rx, jnp.concatenate([back_im] * rx_count, 0), 0.0)
        by_re = dot(weights, wide_re.astype(jnp.bfloat16))
        by_im = dot(weights, wide_im.astype(jnp.bfloat16))
        taps[2 * rx] = by_re[:beam_count] + by_im[beam_count:]
        taps[2 * rx + 1] = by_re[beam_count:] - by_im[:beam_count]

    load.wait()

    def fill_lines(chunk):
        for part in range(2):
            for block in range(per_chunk):
                at = (chunk * per_chunk + block) * LANES
                top = (part * per_chunk + block) * pulses
                for rx in range(rx_count):
                    lines[pl.ds(top, pulses), pl.ds(rx * 2 * LANES, 2 * LANES)] = extended[
                        part, rx, :, pl.ds(at, 2 * LANES)
                    ]

    def fill_filter(beam):
        rows = taps[:, pl.ds(beam, 1), :]
        slanted = pltpu.roll(
            jnp.broadcast_to(rows, (2 * rx_count, 8, 2 * chips)), 0, 2, stride=1, stride_axis=1
        )
        for pair in range(chips // 16):
            first = pltpu.roll(slanted, 16 * pair, 2) if pair else slanted
            second = pltpu.roll(slanted, 16 * pair + 8, 2)
            both = jnp.concatenate([first, second], axis=1).astype(jnp.bfloat16)
            for rx in range(rx_count):
                for part in range(2):
                    for half in range(2):
                        filters[
                            beam,
                            pl.ds(rx * 2 * chips + half * chips + 16 * pair, 16),
                            pl.ds(part * LANES, LANES),
                        ] = both[2 * rx + part, :, half * LANES : (half + 1) * LANES]

    def form_beam(beam):
        mixed = dot(lines[...], filters[beam])
        rows = per_chunk * pulses
        real = mixed[:rows, :LANES] - mixed[rows:, LANES:]
        imag = mixed[rows:, :LANES] + mixed[:rows, LANES:]
        return real.astype(jnp.bfloat16), imag.astype(jnp.bfloat16)

    def put(target, values, top):
        for part in range(2):
            for block in range(per_chunk):
                target[part, pl.ds(top, pulses), pl.ds(block * LANES, LANES)] = values[part][
                    block * pulses : (block + 1) * pulses
                ]

    mine = pl.ds(pl.multiple_of(chan * pulses, pulses), pulses)

    def beam_copy(chunk, beam):
        return pltpu.make_async_remote_copy(
            src_ref=outgoing.at[chunk, beam],
            dst_ref=gathered.at[chunk, :, mine, :],
            send_sem=beam_send.at[chunk],
            recv_sem=beam_recv.at[chunk],
            device_id={"chan": beam},
            device_id_type=MESH,
        )

    def partner(step):
        return lax.rem(chan // 2 + step % 4, chan_count // 2) * 2 + (chan + step // 4) % 2

    fill_lines(0)
    pl.semaphore_wait(barrier, rng_count + chan_count - 2)

    edge = pltpu.make_async_remote_copy(
        src_ref=extended.at[:, :, :, pl.ds(0, LANES)],
        dst_ref=extended.at[:, :, :, pl.ds(gates, LANES)],
        send_sem=edge_sem.at[0],
        recv_sem=edge_sem.at[1],
        device_id={"rng": lax.rem(rng + rng_count - 1, rng_count)},
        device_id_type=MESH,
    )
    edge.start()

    for chunk in range(chunks):
        if chunk:
            if chunk == chunks - 1:
                edge.wait()
                tail = extended[:, :, :, pl.ds(gates, LANES)]
                extended[:, :, :, pl.ds(gates, LANES)] = jnp.where(
                    rng == rng_count - 1, jnp.zeros_like(tail), tail
                )
            fill_lines(chunk)

        @pl.loop(1, chan_count)
        def _(step):
            beam = partner(step)
            if chunk == 0:
                fill_filter(beam)
            put(outgoing.at[chunk, beam], form_beam(beam), 0)
            beam_copy(chunk, beam).start()

        if chunk == 0:
            fill_filter(chan)
        put(gathered.at[chunk], form_beam(chan), pl.multiple_of(chan * pulses, pulses))

    def power_copy(chunk, peer):
        return pltpu.make_async_remote_copy(
            src_ref=power_out.at[chunk, peer],
            dst_ref=power_in.at[chunk, rng],
            send_sem=power_send.at[chunk],
            recv_sem=power_recv.at[chunk],
            device_id={"rng": peer},
            device_id_type=MESH,
        )

    table_load.wait()
    step_bins = 128
    for chunk in range(chunks):
        arrived = outgoing.at[chunk, pl.ds(0, chan_count - 1)]
        pltpu.make_async_copy(arrived, arrived, beam_recv.at[chunk]).wait()
        series = jnp.concatenate([gathered[chunk, 0], gathered[chunk, 1]], axis=0)
        for at in range(0, bins, step_bins):
            real = dot(table[pl.ds(at, step_bins), :], series)
            imag = dot(table[pl.ds(bins + at, step_bins), :], series)
            real = real.astype(jnp.bfloat16).astype(jnp.float32)
            imag = imag.astype(jnp.bfloat16).astype(jnp.float32)
            power = (real * real + imag * imag).reshape(step_bins // own_bins, own_bins, width)
            power = jnp.concatenate(
                [power[:, :, i * LANES : (i + 1) * LANES] for i in range(per_chunk)], axis=1
            )
            power_out[chunk, pl.ds(at // own_bins, step_bins // own_bins)] = power.astype(
                jnp.bfloat16
            )

        @pl.loop(1, rng_count)
        def _(step):
            power_copy(chunk, lax.rem(rng + step, rng_count)).start()

        power_in[chunk, rng] = power_out[chunk, rng]

    total = jnp.zeros((own_bins, LANES), jnp.float32)
    for chunk in range(chunks):
        arrived = power_in.at[chunk, pl.ds(0, rng_count - 1)]
        pltpu.make_async_copy(arrived, arrived, power_recv.at[chunk]).wait()
        level = power_in[chunk].astype(jnp.float32)
        level = jnp.sum(level, axis=0)
        for i in range(per_chunk):
            total = total + level[i * own_bins : (i + 1) * own_bins]
    average = jnp.sum(total, axis=1, keepdims=True) / float(rng_count * gates)
    scale = 1.0 / (average + 1e-06)
    for source in range(rng_count):
        for chunk in range(chunks):
            level = power_in[chunk, source].astype(jnp.float32)
            for i in range(per_chunk):
                out_ref[
                    0, :, pl.ds(source * gates + chunk * width + i * LANES, LANES)
                ] = level[i * own_bins : (i + 1) * own_bins] * scale

    for chunk in range(chunks):
        sent = outgoing.at[chunk, pl.ds(0, chan_count - 1)]
        pltpu.make_async_copy(sent, sent, beam_send.at[chunk]).wait()
        sent = power_out.at[chunk, pl.ds(0, rng_count - 1)]
        pltpu.make_async_copy(sent, sent, power_send.at[chunk]).wait()


def local(rng_count, chan_count, samples, phase_codes, block_pattern, steering):
    _, rx_count, pulses, gates = samples.shape
    chips = phase_codes.shape[1]
    _, beam_count, pair_count = steering.shape
    bins = pulses * chan_count
    own_bins = bins // rng_count
    chunks = 2
    width = gates // chunks
    per_chunk = width // LANES
    vmem = pl.BlockSpec(memory_space=pltpu.VMEM)
    hbm = pl.BlockSpec(memory_space=pl.ANY)
    bf16 = jnp.bfloat16
    return pl.pallas_call(
        functools.partial(kernel, rng_count, chan_count),
        out_shape=jax.ShapeDtypeStruct((1, own_bins, gates * rng_count), jnp.float32),
        in_specs=[hbm, vmem, vmem, vmem, hbm],
        out_specs=vmem,
        scratch_shapes=[
            pltpu.VMEM((2, rx_count, pulses, gates + LANES), bf16),
            pltpu.VMEM((2 * bins, 2 * bins), bf16),
            pltpu.VMEM((2 * rx_count, beam_count, 2 * chips), jnp.float32),
            pltpu.VMEM((beam_count, rx_count * 2 * chips, 2 * LANES), bf16),
            pltpu.VMEM((2 * per_chunk * pulses, rx_count * 2 * LANES), bf16),
            pltpu.VMEM((chunks, beam_count, 2, pulses, width), bf16),
            pltpu.VMEM((chunks, 2, bins, width), bf16),
            pltpu.VMEM((chunks, rng_count, own_bins * per_chunk, LANES), bf16),
            pltpu.VMEM((chunks, rng_count, own_bins * per_chunk, LANES), bf16),
            pltpu.SemaphoreType.DMA,
            pltpu.SemaphoreType.DMA,
            pltpu.SemaphoreType.DMA((2,)),
            pltpu.SemaphoreType.DMA((chunks,)),
            pltpu.SemaphoreType.DMA((chunks,)),
            pltpu.SemaphoreType.DMA((chunks,)),
            pltpu.SemaphoreType.DMA((chunks,)),
        ],
        compiler_params=pltpu.CompilerParams(
            collective_id=0, has_side_effects=True, vmem_limit_bytes=48 * 2**20
        ),
        cost_estimate=pl.CostEstimate(
            flops=3 * 10**9, bytes_accessed=4 * 2**20, transcendentals=0
        ),
    )(
        samples,
        phase_codes,
        block_pattern,
        steering.reshape(2 * beam_count, pair_count),
        dft_table(bins),
    )


def solution(mesh):
    return jax.shard_map(
        functools.partial(local, mesh.shape["rng"], mesh.shape["chan"]),
        mesh=mesh,
        in_specs=(P(None, None, "chan", "rng"), P(), P(), P()),
        out_specs=P("chan", "rng", None),
        check_vma=False,
    )
```

```python
import functools
import math

import jax
import jax.numpy as jnp
import numpy as np
from jax import lax
from jax.experimental import pallas as pl
from jax.experimental.pallas import tpu as pltpu
from jax.sharding import PartitionSpec as P

PHASES = 16
LANES = 128
BLOCKS = (1, 1, 1, 1)
VMEM_BYTES = 64 * 2**20 - 2**17
MESH = pl.DeviceIdType.MESH


def dft_table(pulse_count):
    index = np.arange(pulse_count)
    angles = (np.outer(index, index) % pulse_count) * (2.0 * math.pi / pulse_count)
    cosine, sine = np.cos(angles), np.sin(angles)
    table = np.concatenate(
        [np.concatenate([cosine, sine], axis=1), np.concatenate([-sine, cosine], axis=1)]
    )
    return jnp.asarray(table, jnp.bfloat16)


def dot(left, right):
    return jnp.dot(left, right, preferred_element_type=jnp.float32)


def kernel(
    rng_count,
    chan_count,
    blocks,
    samples_ref,
    codes_hbm,
    pattern_hbm,
    steering_hbm,
    table_hbm,
    out_ref,
    codes_ref,
    pattern_ref,
    steering_ref,
    extended,
    table,
    taps,
    filters,
    lines,
    load_sem,
    edge_sem,
    beam_send,
    beam_recv,
    power_send,
    power_recv,
    *buffers,
):
    rng = lax.axis_index("rng")
    chan = lax.axis_index("chan")
    rx_count, pulses, gates = samples_ref.shape[1:]
    chips = codes_ref.shape[1]
    chunks = len(blocks)
    outgoing, gathered, power_out, power_in = (
        buffers[i * chunks : (i + 1) * chunks] for i in range(4)
    )
    starts = [sum(blocks[:i]) for i in range(chunks)]
    bins = table.shape[0] // 2
    own_bins = bins // rng_count

    small = [
        pltpu.make_async_copy(codes_hbm, codes_ref, load_sem.at[0]),
        pltpu.make_async_copy(pattern_hbm, pattern_ref, load_sem.at[1]),
        pltpu.make_async_copy(steering_hbm, steering_ref, load_sem.at[2]),
    ]
    for copy in small:
        copy.start()
    load = pltpu.make_async_copy(
        samples_ref, extended.at[:, :, :, pl.ds(0, gates)], load_sem.at[3]
    )
    load.start()
    table_load = pltpu.make_async_copy(table_hbm, table, load_sem.at[4])
    table_load.start()

    barrier = pltpu.get_barrier_semaphore()

    @pl.loop(1, chan_count)
    def _(step):
        peer = lax.rem(chan + step, chan_count)
        pl.semaphore_signal(barrier, inc=1, device_id={"chan": peer}, device_id_type=MESH)

    @pl.loop(1, rng_count)
    def _(step):
        peer = lax.rem(rng + step, rng_count)
        pl.semaphore_signal(barrier, inc=1, device_id={"rng": peer}, device_id_type=MESH)

    for copy in small:
        copy.wait()
    block_count, tx_count = pattern_ref.shape
    spread = (
        lax.broadcasted_iota(jnp.int32, (block_count, chips), 1) // (chips // block_count)
        == lax.broadcasted_iota(jnp.int32, (block_count, chips), 0)
    ).astype(jnp.float32)
    active = lax.dot_general(
        pattern_ref[...].astype(jnp.float32),
        spread,
        (((0,), (0,)), ((), ())),
        preferred_element_type=jnp.float32,
    )
    phase = codes_ref[...].astype(jnp.float32) * (2.0 * math.pi / PHASES)
    code_re = (jnp.cos(phase) * active).astype(jnp.bfloat16)
    code_im = (jnp.sin(phase) * active).astype(jnp.bfloat16)
    reverse = (
        lax.rem(
            lax.broadcasted_iota(jnp.int32, (chips, 2 * chips), 0)
            + lax.broadcasted_iota(jnp.int32, (chips, 2 * chips), 1),
            2 * chips,
        )
        == 0
    ).astype(jnp.bfloat16)
    back_re = dot(code_re, reverse)
    back_im = dot(code_im, reverse)
    weights = steering_ref[...]
    beam_count = weights.shape[0] // 2
    row = lax.broadcasted_iota(jnp.int32, (rx_count * tx_count, 2 * chips), 0) // tx_count
    for rx in range(rx_count):
        wide_re = jnp.where(row == rx, jnp.concatenate([back_re] * rx_count, 0), 0.0)
        wide_im = jnp.where(row == rx, jnp.concatenate([back_im] * rx_count, 0), 0.0)
        by_re = dot(weights, wide_re.astype(jnp.bfloat16))
        by_im = dot(weights, wide_im.astype(jnp.bfloat16))
        taps[2 * rx] = by_re[:beam_count] + by_im[beam_count:]
        taps[2 * rx + 1] = by_re[beam_count:] - by_im[:beam_count]

    load.wait()

    def fill_lines(chunk):
        for part in range(2):
            for block in range(blocks[chunk]):
                at = (starts[chunk] + block) * LANES
                top = (part * blocks[chunk] + block) * pulses
                for rx in range(rx_count):
                    lines[pl.ds(top, pulses), pl.ds(rx * 2 * LANES, 2 * LANES)] = extended[
                        part, rx, :, pl.ds(at, 2 * LANES)
                    ]

    def fill_filter(beam):
        rows = taps[:, pl.ds(beam, 1), :]
        slanted = pltpu.roll(
            jnp.broadcast_to(rows, (2 * rx_count, 8, 2 * chips)), 0, 2, stride=1, stride_axis=1
        )
        for pair in range(chips // 16):
            first = pltpu.roll(slanted, 16 * pair, 2) if pair else slanted
            second = pltpu.roll(slanted, 16 * pair + 8, 2)
            both = jnp.concatenate([first, second], axis=1).astype(jnp.bfloat16)
            for rx in range(rx_count):
                for part in range(2):
                    for half in range(2):
                        filters[
                            beam,
                            pl.ds(rx * 2 * chips + half * chips + 16 * pair, 16),
                            pl.ds(part * LANES, LANES),
                        ] = both[2 * rx + part, :, half * LANES : (half + 1) * LANES]

    def form_beam(chunk, beam):
        rows = blocks[chunk] * pulses
        mixed = dot(lines[pl.ds(0, 2 * rows), :], filters[beam])
        real = mixed[:rows, :LANES] - mixed[rows:, LANES:]
        imag = mixed[rows:, :LANES] + mixed[:rows, LANES:]
        return real.astype(jnp.bfloat16), imag.astype(jnp.bfloat16)

    def put(chunk, target, values, top):
        for part in range(2):
            for block in range(blocks[chunk]):
                target[part, pl.ds(top, pulses), pl.ds(block * LANES, LANES)] = values[part][
                    block * pulses : (block + 1) * pulses
                ]

    mine = pl.ds(pl.multiple_of(chan * pulses, pulses), pulses)

    def beam_copy(chunk, beam):
        return pltpu.make_async_remote_copy(
            src_ref=outgoing[chunk].at[beam],
            dst_ref=gathered[chunk].at[:, mine, :],
            send_sem=beam_send.at[chunk],
            recv_sem=beam_recv.at[chunk],
            device_id={"chan": beam},
            device_id_type=MESH,
        )

    def partner(step):
        return lax.rem(chan // 2 + step % 4, chan_count // 2) * 2 + (chan + step // 4) % 2

    fill_lines(0)
    pl.semaphore_wait(barrier, rng_count + chan_count - 2)

    edge = pltpu.make_async_remote_copy(
        src_ref=extended.at[:, :, :, pl.ds(0, LANES)],
        dst_ref=extended.at[:, :, :, pl.ds(gates, LANES)],
        send_sem=edge_sem.at[0],
        recv_sem=edge_sem.at[1],
        device_id={"rng": lax.rem(rng + rng_count - 1, rng_count)},
        device_id_type=MESH,
    )
    edge.start()

    for chunk in range(chunks):
        if chunk:
            if chunk == chunks - 1:
                edge.wait()
                tail = extended[:, :, :, pl.ds(gates, LANES)]
                extended[:, :, :, pl.ds(gates, LANES)] = jnp.where(
                    rng == rng_count - 1, jnp.zeros_like(tail), tail
                )
            fill_lines(chunk)

        @pl.loop(1, chan_count)
        def _(step):
            beam = partner(step)
            if chunk == 0:
                fill_filter(beam)
            put(chunk, outgoing[chunk].at[beam], form_beam(chunk, beam), 0)
            beam_copy(chunk, beam).start()

        if chunk == 0:
            fill_filter(chan)
        put(chunk, gathered[chunk], form_beam(chunk, chan), pl.multiple_of(chan * pulses, pulses))

    def power_copy(chunk, peer):
        return pltpu.make_async_remote_copy(
            src_ref=power_out[chunk].at[peer],
            dst_ref=power_in[chunk].at[rng],
            send_sem=power_send.at[chunk],
            recv_sem=power_recv.at[chunk],
            device_id={"rng": peer},
            device_id_type=MESH,
        )

    table_load.wait()
    step_bins = 128
    for chunk in range(chunks):
        arrived = outgoing[chunk].at[pl.ds(0, chan_count - 1)]
        pltpu.make_async_copy(arrived, arrived, beam_recv.at[chunk]).wait()
        series = jnp.concatenate([gathered[chunk][0], gathered[chunk][1]], axis=0)
        for at in range(0, bins, step_bins):
            real = dot(table[pl.ds(at, step_bins), :], series)
            imag = dot(table[pl.ds(bins + at, step_bins), :], series)
            real = real.astype(jnp.bfloat16).astype(jnp.float32)
            imag = imag.astype(jnp.bfloat16).astype(jnp.float32)
            power = (real * real + imag * imag).reshape(
                step_bins // own_bins, own_bins, blocks[chunk] * LANES
            )
            power = jnp.concatenate(
                [power[:, :, i * LANES : (i + 1) * LANES] for i in range(blocks[chunk])], axis=1
            )
            power_out[chunk][pl.ds(at // own_bins, step_bins // own_bins)] = power.astype(
                jnp.bfloat16
            )

        @pl.loop(1, rng_count)
        def _(step):
            power_copy(chunk, lax.rem(rng + step, rng_count)).start()

        power_in[chunk][rng] = power_out[chunk][rng]

    total = jnp.zeros((own_bins, LANES), jnp.float32)
    for chunk in range(chunks):
        arrived = power_in[chunk].at[pl.ds(0, rng_count - 1)]
        pltpu.make_async_copy(arrived, arrived, power_recv.at[chunk]).wait()
        level = jnp.sum(power_in[chunk][...].astype(jnp.float32), axis=0)
        for i in range(blocks[chunk]):
            total = total + level[i * own_bins : (i + 1) * own_bins]
    average = jnp.sum(total, axis=1, keepdims=True) / float(rng_count * gates)
    scale = 1.0 / (average + 1e-06)
    for source in range(rng_count):
        for chunk in range(chunks):
            level = power_in[chunk][source].astype(jnp.float32)
            for i in range(blocks[chunk]):
                out_ref[
                    0, :, pl.ds(source * gates + (starts[chunk] + i) * LANES, LANES)
                ] = level[i * own_bins : (i + 1) * own_bins] * scale

    for chunk in range(chunks):
        sent = outgoing[chunk].at[pl.ds(0, chan_count - 1)]
        pltpu.make_async_copy(sent, sent, beam_send.at[chunk]).wait()
        sent = power_out[chunk].at[pl.ds(0, rng_count - 1)]
        pltpu.make_async_copy(sent, sent, power_send.at[chunk]).wait()


def local(rng_count, chan_count, samples, phase_codes, block_pattern, steering):
    _, rx_count, pulses, gates = samples.shape
    chips = phase_codes.shape[1]
    _, beam_count, pair_count = steering.shape
    bins = pulses * chan_count
    own_bins = bins // rng_count
    blocks = BLOCKS
    chunks = len(blocks)
    vmem = pl.BlockSpec(memory_space=pltpu.VMEM)
    hbm = pl.BlockSpec(memory_space=pltpu.HBM)
    bf16 = jnp.bfloat16
    return pl.pallas_call(
        functools.partial(kernel, rng_count, chan_count, blocks),
        out_shape=jax.ShapeDtypeStruct((1, own_bins, gates * rng_count), jnp.float32),
        in_specs=[hbm] * 5,
        out_specs=vmem,
        scratch_shapes=[
            pltpu.VMEM(phase_codes.shape, jnp.int32),
            pltpu.VMEM(block_pattern.shape[::-1], jnp.int32),
            pltpu.VMEM((2 * beam_count, pair_count), bf16),
            pltpu.VMEM((2, rx_count, pulses, gates + LANES), bf16),
            pltpu.VMEM((2 * bins, 2 * bins), bf16),
            pltpu.VMEM((2 * rx_count, beam_count, 2 * chips), jnp.float32),
            pltpu.VMEM((beam_count, rx_count * 2 * chips, 2 * LANES), bf16),
            pltpu.VMEM((2 * max(blocks) * pulses, rx_count * 2 * LANES), bf16),
            pltpu.SemaphoreType.DMA((5,)),
            pltpu.SemaphoreType.DMA((2,)),
            pltpu.SemaphoreType.DMA((chunks,)),
            pltpu.SemaphoreType.DMA((chunks,)),
            pltpu.SemaphoreType.DMA((chunks,)),
            pltpu.SemaphoreType.DMA((chunks,)),
            *(pltpu.VMEM((beam_count, 2, pulses, n * LANES), bf16) for n in blocks),
            *(pltpu.VMEM((2, bins, n * LANES), bf16) for n in blocks),
            *(pltpu.VMEM((rng_count, own_bins * n, LANES), bf16) for n in blocks * 2),
        ],
        compiler_params=pltpu.CompilerParams(
            collective_id=0, has_side_effects=True, vmem_limit_bytes=VMEM_BYTES
        ),
        cost_estimate=pl.CostEstimate(
            flops=3 * 10**9, bytes_accessed=4 * 2**20, transcendentals=0
        ),
    )(
        samples,
        phase_codes,
        block_pattern.T,
        steering.reshape(2 * beam_count, pair_count),
        dft_table(bins),
    )


def solution(mesh):
    return jax.shard_map(
        functools.partial(local, mesh.shape["rng"], mesh.shape["chan"]),
        mesh=mesh,
        in_specs=(P(None, None, "chan", "rng"), P(), P(), P()),
        out_specs=P("chan", "rng", None),
        check_vma=False,
    )
```

```python
import functools
import math

import jax
import jax.numpy as jnp
import numpy as np
from jax import lax
from jax.experimental import pallas as pl
from jax.experimental.pallas import tpu as pltpu
from jax.sharding import PartitionSpec as P

PHASES = 16
LANES = 128
BLOCKS = (1, 1, 1, 1)
STEPS = 2
VMEM_BYTES = 64 * 2**20 - 2**17
MESH = pl.DeviceIdType.MESH


def dft_table(pulse_count):
    index = np.arange(pulse_count)
    angles = (np.outer(index, index) % pulse_count) * (2.0 * math.pi / pulse_count)
    cosine, sine = np.cos(angles), np.sin(angles)
    table = np.concatenate(
        [np.concatenate([cosine, sine], axis=1), np.concatenate([-sine, cosine], axis=1)]
    )
    return jnp.asarray(table, jnp.bfloat16)


def dot(left, right):
    return jnp.dot(left, right, preferred_element_type=jnp.float32)


def kernel(
    rng_count,
    chan_count,
    blocks,
    samples_ref,
    codes_hbm,
    pattern_hbm,
    steering_hbm,
    table_hbm,
    *refs,
):
    levels, scale_hbm = refs[: len(blocks)], refs[len(blocks)]
    (
        codes_ref,
        pattern_ref,
        steering_ref,
        extended,
        table,
        taps,
        filters,
        lines,
        load_sem,
        edge_sem,
        beam_send,
        beam_recv,
        power_send,
        power_recv,
        scale,
        scale_sem,
        *buffers,
    ) = refs[len(blocks) + 1 :]
    rng = lax.axis_index("rng")
    chan = lax.axis_index("chan")
    rx_count, pulses, gates = samples_ref.shape[1:]
    chips = codes_ref.shape[1]
    chunks = len(blocks)
    outgoing, gathered, power_out, power_in = (
        buffers[i * chunks : (i + 1) * chunks] for i in range(4)
    )
    starts = [sum(blocks[:i]) for i in range(chunks)]
    bins = table.shape[0] // 2
    own_bins = bins // rng_count

    small = [
        pltpu.make_async_copy(codes_hbm, codes_ref, load_sem.at[0]),
        pltpu.make_async_copy(pattern_hbm, pattern_ref, load_sem.at[1]),
        pltpu.make_async_copy(steering_hbm, steering_ref, load_sem.at[2]),
    ]
    for copy in small:
        copy.start()
    load = pltpu.make_async_copy(
        samples_ref, extended.at[:, :, :, pl.ds(0, gates)], load_sem.at[3]
    )
    load.start()
    table_load = pltpu.make_async_copy(table_hbm, table, load_sem.at[4])
    table_load.start()

    barrier = pltpu.get_barrier_semaphore()

    @pl.loop(1, chan_count)
    def _(step):
        peer = lax.rem(chan + step, chan_count)
        pl.semaphore_signal(barrier, inc=1, device_id={"chan": peer}, device_id_type=MESH)

    @pl.loop(1, rng_count)
    def _(step):
        peer = lax.rem(rng + step, rng_count)
        pl.semaphore_signal(barrier, inc=1, device_id={"rng": peer}, device_id_type=MESH)

    for copy in small:
        copy.wait()
    block_count, tx_count = pattern_ref.shape
    spread = (
        lax.broadcasted_iota(jnp.int32, (block_count, chips), 1) // (chips // block_count)
        == lax.broadcasted_iota(jnp.int32, (block_count, chips), 0)
    ).astype(jnp.float32)
    active = lax.dot_general(
        pattern_ref[...].astype(jnp.float32),
        spread,
        (((0,), (0,)), ((), ())),
        preferred_element_type=jnp.float32,
    )
    phase = codes_ref[...].astype(jnp.float32) * (2.0 * math.pi / PHASES)
    code_re = (jnp.cos(phase) * active).astype(jnp.bfloat16)
    code_im = (jnp.sin(phase) * active).astype(jnp.bfloat16)
    reverse = (
        lax.rem(
            lax.broadcasted_iota(jnp.int32, (chips, 2 * chips), 0)
            + lax.broadcasted_iota(jnp.int32, (chips, 2 * chips), 1),
            2 * chips,
        )
        == 0
    ).astype(jnp.bfloat16)
    back_re = dot(code_re, reverse)
    back_im = dot(code_im, reverse)
    weights = steering_ref[...]
    beam_count = weights.shape[0] // 2
    row = lax.broadcasted_iota(jnp.int32, (rx_count * tx_count, 2 * chips), 0) // tx_count
    for rx in range(rx_count):
        wide_re = jnp.where(row == rx, jnp.concatenate([back_re] * rx_count, 0), 0.0)
        wide_im = jnp.where(row == rx, jnp.concatenate([back_im] * rx_count, 0), 0.0)
        by_re = dot(weights, wide_re.astype(jnp.bfloat16))
        by_im = dot(weights, wide_im.astype(jnp.bfloat16))
        taps[2 * rx] = by_re[:beam_count] + by_im[beam_count:]
        taps[2 * rx + 1] = by_re[beam_count:] - by_im[:beam_count]

    load.wait()

    def fill_lines(chunk):
        for part in range(2):
            for block in range(blocks[chunk]):
                at = (starts[chunk] + block) * LANES
                top = (part * blocks[chunk] + block) * pulses
                for rx in range(rx_count):
                    lines[pl.ds(top, pulses), pl.ds(rx * 2 * LANES, 2 * LANES)] = extended[
                        part, rx, :, pl.ds(at, 2 * LANES)
                    ]

    def fill_filter(beam):
        rows = taps[:, pl.ds(beam, 1), :]
        slanted = pltpu.roll(
            jnp.broadcast_to(rows, (2 * rx_count, 8, 2 * chips)), 0, 2, stride=1, stride_axis=1
        )
        for pair in range(chips // 16):
            first = pltpu.roll(slanted, 16 * pair, 2) if pair else slanted
            second = pltpu.roll(slanted, 16 * pair + 8, 2)
            both = jnp.concatenate([first, second], axis=1).astype(jnp.bfloat16)
            for rx in range(rx_count):
                for part in range(2):
                    for half in range(2):
                        filters[
                            beam,
                            pl.ds(rx * 2 * chips + half * chips + 16 * pair, 16),
                            pl.ds(part * LANES, LANES),
                        ] = both[2 * rx + part, :, half * LANES : (half + 1) * LANES]

    def form_beam(chunk, beam):
        rows = blocks[chunk] * pulses
        mixed = dot(lines[pl.ds(0, 2 * rows), :], filters[beam])
        real = mixed[:rows, :LANES] - mixed[rows:, LANES:]
        imag = mixed[rows:, :LANES] + mixed[:rows, LANES:]
        return real.astype(jnp.bfloat16), imag.astype(jnp.bfloat16)

    def put(chunk, target, values, top):
        for part in range(2):
            for block in range(blocks[chunk]):
                target[part, pl.ds(top, pulses), pl.ds(block * LANES, LANES)] = values[part][
                    block * pulses : (block + 1) * pulses
                ]

    mine = pl.ds(pl.multiple_of(chan * pulses, pulses), pulses)

    def beam_copy(chunk, beam):
        return pltpu.make_async_remote_copy(
            src_ref=outgoing[chunk].at[beam],
            dst_ref=gathered[chunk].at[:, mine, :],
            send_sem=beam_send.at[chunk],
            recv_sem=beam_recv.at[chunk],
            device_id={"chan": beam},
            device_id_type=MESH,
        )

    def partner(step):
        return lax.rem(chan // 2 + step % 4, chan_count // 2) * 2 + (chan + step // 4) % 2

    fill_lines(0)
    pl.semaphore_wait(barrier, rng_count + chan_count - 2)

    edge = pltpu.make_async_remote_copy(
        src_ref=extended.at[:, :, :, pl.ds(0, LANES)],
        dst_ref=extended.at[:, :, :, pl.ds(gates, LANES)],
        send_sem=edge_sem.at[0],
        recv_sem=edge_sem.at[1],
        device_id={"rng": lax.rem(rng + rng_count - 1, rng_count)},
        device_id_type=MESH,
    )
    edge.start()

    for chunk in range(chunks):
        if chunk:
            if chunk == chunks - 1:
                edge.wait()
                tail = extended[:, :, :, pl.ds(gates, LANES)]
                extended[:, :, :, pl.ds(gates, LANES)] = jnp.where(
                    rng == rng_count - 1, jnp.zeros_like(tail), tail
                )
            fill_lines(chunk)

        @pl.loop(1, chan_count)
        def _(step):
            beam = partner(step)
            if chunk == 0:
                fill_filter(beam)
            put(chunk, outgoing[chunk].at[beam], form_beam(chunk, beam), 0)
            beam_copy(chunk, beam).start()

        if chunk == 0:
            fill_filter(chan)
        put(chunk, gathered[chunk], form_beam(chunk, chan), pl.multiple_of(chan * pulses, pulses))

    def power_copy(chunk, peer):
        return pltpu.make_async_remote_copy(
            src_ref=power_out[chunk].at[peer],
            dst_ref=power_in[chunk].at[rng],
            send_sem=power_send.at[chunk],
            recv_sem=power_recv.at[chunk],
            device_id={"rng": peer},
            device_id_type=MESH,
        )

    table_load.wait()
    step_bins = 128
    for chunk in range(chunks):
        arrived = outgoing[chunk].at[pl.ds(0, chan_count - 1)]
        pltpu.make_async_copy(arrived, arrived, beam_recv.at[chunk]).wait()
        series = jnp.concatenate([gathered[chunk][0], gathered[chunk][1]], axis=0)
        for at in range(0, bins, step_bins):
            real = dot(table[pl.ds(at, step_bins), :], series)
            imag = dot(table[pl.ds(bins + at, step_bins), :], series)
            real = real.astype(jnp.bfloat16).astype(jnp.float32)
            imag = imag.astype(jnp.bfloat16).astype(jnp.float32)
            power = (real * real + imag * imag).reshape(
                step_bins // own_bins, own_bins, blocks[chunk] * LANES
            )
            power = jnp.concatenate(
                [power[:, :, i * LANES : (i + 1) * LANES] for i in range(blocks[chunk])], axis=1
            )
            power_out[chunk][pl.ds(at // own_bins, step_bins // own_bins)] = power.astype(
                jnp.bfloat16
            )

        @pl.loop(1, rng_count, unroll=7)
        def _(step):
            power_copy(chunk, lax.rem(rng + step, rng_count)).start()

        power_in[chunk][rng] = power_out[chunk][rng]

    total = jnp.zeros((own_bins, LANES), jnp.float32)
    for chunk in range(chunks):
        arrived = power_in[chunk].at[pl.ds(0, rng_count - 1)]
        pltpu.make_async_copy(arrived, arrived, power_recv.at[chunk]).wait()
        pltpu.make_async_copy(power_in[chunk], levels[chunk], load_sem.at[chunk]).start()
        level = jnp.sum(power_in[chunk][...].astype(jnp.float32), axis=0)
        for i in range(blocks[chunk]):
            total = total + level[i * own_bins : (i + 1) * own_bins]
    average = jnp.sum(total, axis=1, keepdims=True) / float(rng_count * gates)
    scale[...] = jnp.broadcast_to(1.0 / (average + 1e-06), scale.shape)
    scale_store = pltpu.make_async_copy(scale, scale_hbm, scale_sem)
    scale_store.start()
    for chunk in range(chunks):
        sent = outgoing[chunk].at[pl.ds(0, chan_count - 1)]
        pltpu.make_async_copy(sent, sent, beam_send.at[chunk]).wait()
        sent = power_out[chunk].at[pl.ds(0, rng_count - 1)]
        pltpu.make_async_copy(sent, sent, power_send.at[chunk]).wait()
        pltpu.make_async_copy(power_in[chunk], levels[chunk], load_sem.at[chunk]).wait()
    scale_store.wait()


def finish(blocks, *refs):
    levels, scale_ref, out_ref = refs[:-2], refs[-2], refs[-1]
    sources, _, lanes = levels[0].shape
    own_bins = out_ref.shape[1]
    scale = scale_ref[...]
    at = 0
    for source in range(sources):
        for n, ref in zip(blocks, levels, strict=True):
            level = ref[source].astype(jnp.float32)
            for i in range(n):
                out_ref[0, :, pl.ds(at, lanes)] = level[i * own_bins : (i + 1) * own_bins] * scale
                at += lanes


def local(rng_count, chan_count, samples, phase_codes, block_pattern, steering):
    _, rx_count, pulses, gates = samples.shape
    chips = phase_codes.shape[1]
    _, beam_count, pair_count = steering.shape
    bins = pulses * chan_count
    own_bins = bins // rng_count
    blocks = BLOCKS
    chunks = len(blocks)
    vmem = pl.BlockSpec(memory_space=pltpu.VMEM)
    hbm = pl.BlockSpec(memory_space=pltpu.HBM)
    bf16 = jnp.bfloat16
    levels = pl.pallas_call(
        functools.partial(kernel, rng_count, chan_count, blocks),
        out_shape=[
            jax.ShapeDtypeStruct((rng_count, own_bins * n, LANES), bf16) for n in blocks
        ]
        + [jax.ShapeDtypeStruct((own_bins, LANES), jnp.float32)],
        in_specs=[hbm] * 5,
        out_specs=[hbm] * (chunks + 1),
        scratch_shapes=[
            pltpu.VMEM(phase_codes.shape, jnp.int32),
            pltpu.VMEM(block_pattern.shape[::-1], jnp.int32),
            pltpu.VMEM((2 * beam_count, pair_count), bf16),
            pltpu.VMEM((2, rx_count, pulses, gates + LANES), bf16),
            pltpu.VMEM((2 * bins, 2 * bins), bf16),
            pltpu.VMEM((2 * rx_count, beam_count, 2 * chips), jnp.float32),
            pltpu.VMEM((beam_count, rx_count * 2 * chips, 2 * LANES), bf16),
            pltpu.VMEM((2 * max(blocks) * pulses, rx_count * 2 * LANES), bf16),
            pltpu.SemaphoreType.DMA((5,)),
            pltpu.SemaphoreType.DMA((2,)),
            pltpu.SemaphoreType.DMA((chunks,)),
            pltpu.SemaphoreType.DMA((chunks,)),
            pltpu.SemaphoreType.DMA((chunks,)),
            pltpu.SemaphoreType.DMA((chunks,)),
            pltpu.VMEM((own_bins, LANES), jnp.float32),
            pltpu.SemaphoreType.DMA,
            *(pltpu.VMEM((beam_count, 2, pulses, n * LANES), bf16) for n in blocks),
            *(pltpu.VMEM((2, bins, n * LANES), bf16) for n in blocks),
            *(pltpu.VMEM((rng_count, own_bins * n, LANES), bf16) for n in blocks * 2),
        ],
        compiler_params=pltpu.CompilerParams(
            collective_id=0, has_side_effects=True, vmem_limit_bytes=VMEM_BYTES
        ),
        cost_estimate=pl.CostEstimate(
            flops=3 * 10**9, bytes_accessed=4 * 2**20, transcendentals=0
        ),
    )(
        samples,
        phase_codes,
        block_pattern.T,
        steering.reshape(2 * beam_count, pair_count),
        dft_table(bins),
    )
    return pl.pallas_call(
        functools.partial(finish, blocks),
        out_shape=jax.ShapeDtypeStruct((1, own_bins, gates * rng_count), jnp.float32),
        grid=(STEPS,),
        in_specs=[
            pl.BlockSpec((rng_count // STEPS, own_bins * n, LANES), lambda i: (i, 0, 0))
            for n in blocks
        ]
        + [pl.BlockSpec((own_bins, LANES), lambda i: (0, 0))],
        out_specs=pl.BlockSpec((1, own_bins, gates * rng_count // STEPS), lambda i: (0, 0, i)),
    )(*levels)


def solution(mesh):
    return jax.shard_map(
        functools.partial(local, mesh.shape["rng"], mesh.shape["chan"]),
        mesh=mesh,
        in_specs=(P(None, None, "chan", "rng"), P(), P(), P()),
        out_specs=P("chan", "rng", None),
        check_vma=False,
    )
```

```python
import functools
import math

import jax
import jax.numpy as jnp
import numpy as np
from jax import lax
from jax.experimental import pallas as pl
from jax.experimental.pallas import tpu as pltpu
from jax.sharding import PartitionSpec as P

PHASES = 16
LANES = 128
BLOCKS = (1, 1, 1, 1)
STEPS = 2
VMEM_BYTES = 64 * 2**20 - 2**17
MESH = pl.DeviceIdType.MESH


def dft_table(pulse_count):
    index = np.arange(pulse_count)
    angles = (np.outer(index, index) % pulse_count) * (2.0 * math.pi / pulse_count)
    cosine, sine = np.cos(angles), np.sin(angles)
    table = np.concatenate(
        [np.concatenate([cosine, sine], axis=1), np.concatenate([-sine, cosine], axis=1)]
    )
    return jnp.asarray(table, jnp.bfloat16)


def dot(left, right):
    return jnp.dot(left, right, preferred_element_type=jnp.float32)


def kernel(
    rng_count,
    chan_count,
    blocks,
    samples_ref,
    codes_hbm,
    pattern_hbm,
    steering_hbm,
    table_hbm,
    *refs,
):
    levels, scale_hbm = refs[: len(blocks)], refs[len(blocks)]
    (
        codes_ref,
        pattern_ref,
        steering_ref,
        extended,
        table,
        taps,
        filters,
        lines,
        load_sem,
        edge_sem,
        beam_send,
        beam_recv,
        power_send,
        power_recv,
        scale,
        scale_sem,
        *buffers,
    ) = refs[len(blocks) + 1 :]
    rng = lax.axis_index("rng")
    chan = lax.axis_index("chan")
    rx_count, pulses, gates = samples_ref.shape[1:]
    chips = codes_ref.shape[1]
    chunks = len(blocks)
    outgoing, gathered, power_out, power_in = (
        buffers[i * chunks : (i + 1) * chunks] for i in range(4)
    )
    starts = [sum(blocks[:i]) for i in range(chunks)]
    bins = table.shape[0] // 2
    own_bins = bins // rng_count

    small = [
        pltpu.make_async_copy(codes_hbm, codes_ref, load_sem.at[0]),
        pltpu.make_async_copy(pattern_hbm, pattern_ref, load_sem.at[1]),
        pltpu.make_async_copy(steering_hbm, steering_ref, load_sem.at[2]),
    ]
    for copy in small:
        copy.start()
    load = pltpu.make_async_copy(
        samples_ref, extended.at[:, :, :, pl.ds(0, gates)], load_sem.at[3]
    )
    load.start()
    table_load = pltpu.make_async_copy(table_hbm, table, load_sem.at[4])
    table_load.start()

    barrier = pltpu.get_barrier_semaphore()

    @pl.loop(1, chan_count)
    def _(step):
        peer = lax.rem(chan + step, chan_count)
        pl.semaphore_signal(barrier, inc=1, device_id={"chan": peer}, device_id_type=MESH)

    @pl.loop(1, rng_count)
    def _(step):
        peer = lax.rem(rng + step, rng_count)
        pl.semaphore_signal(barrier, inc=1, device_id={"rng": peer}, device_id_type=MESH)

    for copy in small:
        copy.wait()
    block_count, tx_count = pattern_ref.shape
    spread = (
        lax.broadcasted_iota(jnp.int32, (block_count, chips), 1) // (chips // block_count)
        == lax.broadcasted_iota(jnp.int32, (block_count, chips), 0)
    ).astype(jnp.float32)
    active = lax.dot_general(
        pattern_ref[...].astype(jnp.float32),
        spread,
        (((0,), (0,)), ((), ())),
        preferred_element_type=jnp.float32,
    )
    phase = codes_ref[...].astype(jnp.float32) * (2.0 * math.pi / PHASES)
    code_re = (jnp.cos(phase) * active).astype(jnp.bfloat16)
    code_im = (jnp.sin(phase) * active).astype(jnp.bfloat16)
    reverse = (
        lax.rem(
            lax.broadcasted_iota(jnp.int32, (chips, 2 * chips), 0)
            + lax.broadcasted_iota(jnp.int32, (chips, 2 * chips), 1),
            2 * chips,
        )
        == 0
    ).astype(jnp.bfloat16)
    back_re = dot(code_re, reverse)
    back_im = dot(code_im, reverse)
    weights = steering_ref[...]
    beam_count = weights.shape[0] // 2
    row = lax.broadcasted_iota(jnp.int32, (rx_count * tx_count, 2 * chips), 0) // tx_count
    for rx in range(rx_count):
        wide_re = jnp.where(row == rx, jnp.concatenate([back_re] * rx_count, 0), 0.0)
        wide_im = jnp.where(row == rx, jnp.concatenate([back_im] * rx_count, 0), 0.0)
        by_re = dot(weights, wide_re.astype(jnp.bfloat16))
        by_im = dot(weights, wide_im.astype(jnp.bfloat16))
        taps[2 * rx] = by_re[:beam_count] + by_im[beam_count:]
        taps[2 * rx + 1] = by_re[beam_count:] - by_im[:beam_count]

    load.wait()

    def fill_lines(chunk):
        for part in range(2):
            for block in range(blocks[chunk]):
                at = (starts[chunk] + block) * LANES
                top = (part * blocks[chunk] + block) * pulses
                for rx in range(rx_count):
                    lines[pl.ds(top, pulses), pl.ds(rx * 2 * LANES, 2 * LANES)] = extended[
                        part, rx, :, pl.ds(at, 2 * LANES)
                    ]

    def fill_filter(beam):
        rows = taps[:, pl.ds(beam, 1), :]
        slanted = pltpu.roll(
            jnp.broadcast_to(rows, (2 * rx_count, 8, 2 * chips)), 0, 2, stride=1, stride_axis=1
        )
        for pair in range(chips // 16):
            first = pltpu.roll(slanted, 16 * pair, 2) if pair else slanted
            second = pltpu.roll(slanted, 16 * pair + 8, 2)
            both = jnp.concatenate([first, second], axis=1).astype(jnp.bfloat16)
            for rx in range(rx_count):
                for part in range(2):
                    for half in range(2):
                        filters[
                            beam,
                            pl.ds(rx * 2 * chips + half * chips + 16 * pair, 16),
                            pl.ds(part * LANES, LANES),
                        ] = both[2 * rx + part, :, half * LANES : (half + 1) * LANES]

    def form_beam(chunk, beam):
        rows = blocks[chunk] * pulses
        mixed = dot(lines[pl.ds(0, 2 * rows), :], filters[beam])
        real = mixed[:rows, :LANES] - mixed[rows:, LANES:]
        imag = mixed[rows:, :LANES] + mixed[:rows, LANES:]
        return real.astype(jnp.bfloat16), imag.astype(jnp.bfloat16)

    def put(chunk, target, values, top):
        for part in range(2):
            for block in range(blocks[chunk]):
                target[part, pl.ds(top, pulses), pl.ds(block * LANES, LANES)] = values[part][
                    block * pulses : (block + 1) * pulses
                ]

    mine = pl.ds(pl.multiple_of(chan * pulses, pulses), pulses)

    def beam_copy(chunk, beam):
        return pltpu.make_async_remote_copy(
            src_ref=outgoing[chunk].at[beam],
            dst_ref=gathered[chunk].at[:, mine, :],
            send_sem=beam_send.at[chunk],
            recv_sem=beam_recv.at[chunk],
            device_id={"chan": beam},
            device_id_type=MESH,
        )

    def partner(step):
        pair = (step - 1) // 2
        turn = jnp.where(pair == 0, 1, jnp.where(pair == 1, 3, jnp.where(pair == 2, 2, 0)))
        flip = jnp.where(pair == 3, 1, (step - 1) % 2)
        return lax.rem(chan // 2 + turn, chan_count // 2) * 2 + (chan + flip) % 2

    fill_lines(0)
    pl.semaphore_wait(barrier, rng_count + chan_count - 2)

    edge = pltpu.make_async_remote_copy(
        src_ref=extended.at[:, :, :, pl.ds(0, LANES)],
        dst_ref=extended.at[:, :, :, pl.ds(gates, LANES)],
        send_sem=edge_sem.at[0],
        recv_sem=edge_sem.at[1],
        device_id={"rng": lax.rem(rng + rng_count - 1, rng_count)},
        device_id_type=MESH,
    )
    edge.start()

    for chunk in range(chunks):
        if chunk:
            if chunk == chunks - 1:
                edge.wait()
                tail = extended[:, :, :, pl.ds(gates, LANES)]
                extended[:, :, :, pl.ds(gates, LANES)] = jnp.where(
                    rng == rng_count - 1, jnp.zeros_like(tail), tail
                )
            fill_lines(chunk)

        @pl.loop(1, chan_count)
        def _(step):
            beam = partner(step)
            if chunk == 0:
                fill_filter(beam)
            put(chunk, outgoing[chunk].at[beam], form_beam(chunk, beam), 0)
            beam_copy(chunk, beam).start()

        if chunk == 0:
            fill_filter(chan)
        put(chunk, gathered[chunk], form_beam(chunk, chan), pl.multiple_of(chan * pulses, pulses))

    def power_copy(chunk, peer):
        return pltpu.make_async_remote_copy(
            src_ref=power_out[chunk].at[peer],
            dst_ref=power_in[chunk].at[rng],
            send_sem=power_send.at[chunk],
            recv_sem=power_recv.at[chunk],
            device_id={"rng": peer},
            device_id_type=MESH,
        )

    table_load.wait()
    step_bins = 128
    for chunk in range(chunks):
        arrived = outgoing[chunk].at[pl.ds(0, chan_count - 1)]
        pltpu.make_async_copy(arrived, arrived, beam_recv.at[chunk]).wait()
        series = jnp.concatenate([gathered[chunk][0], gathered[chunk][1]], axis=0)
        for at in range(0, bins, step_bins):
            real = dot(table[pl.ds(at, step_bins), :], series)
            imag = dot(table[pl.ds(bins + at, step_bins), :], series)
            real = real.astype(jnp.bfloat16).astype(jnp.float32)
            imag = imag.astype(jnp.bfloat16).astype(jnp.float32)
            power = (real * real + imag * imag).reshape(
                step_bins // own_bins, own_bins, blocks[chunk] * LANES
            )
            power = jnp.concatenate(
                [power[:, :, i * LANES : (i + 1) * LANES] for i in range(blocks[chunk])], axis=1
            )
            power_out[chunk][pl.ds(at // own_bins, step_bins // own_bins)] = power.astype(
                jnp.bfloat16
            )

        @pl.loop(1, rng_count, unroll=7)
        def _(step):
            power_copy(chunk, lax.rem(rng + step, rng_count)).start()

        power_in[chunk][rng] = power_out[chunk][rng]

    total = jnp.zeros((own_bins, LANES), jnp.float32)
    for chunk in range(chunks):
        arrived = power_in[chunk].at[pl.ds(0, rng_count - 1)]
        pltpu.make_async_copy(arrived, arrived, power_recv.at[chunk]).wait()
        pltpu.make_async_copy(power_in[chunk], levels[chunk], load_sem.at[chunk]).start()
        level = jnp.sum(power_in[chunk][...].astype(jnp.float32), axis=0)
        for i in range(blocks[chunk]):
            total = total + level[i * own_bins : (i + 1) * own_bins]
    average = jnp.sum(total, axis=1, keepdims=True) / float(rng_count * gates)
    scale[...] = jnp.broadcast_to(1.0 / (average + 1e-06), scale.shape)
    scale_store = pltpu.make_async_copy(scale, scale_hbm, scale_sem)
    scale_store.start()
    for chunk in range(chunks):
        sent = outgoing[chunk].at[pl.ds(0, chan_count - 1)]
        pltpu.make_async_copy(sent, sent, beam_send.at[chunk]).wait()
        sent = power_out[chunk].at[pl.ds(0, rng_count - 1)]
        pltpu.make_async_copy(sent, sent, power_send.at[chunk]).wait()
        pltpu.make_async_copy(power_in[chunk], levels[chunk], load_sem.at[chunk]).wait()
    scale_store.wait()


def finish(blocks, *refs):
    levels, scale_ref, out_ref = refs[:-2], refs[-2], refs[-1]
    sources, _, lanes = levels[0].shape
    own_bins = out_ref.shape[1]
    scale = scale_ref[...]
    at = 0
    for source in range(sources):
        for n, ref in zip(blocks, levels, strict=True):
            level = ref[source].astype(jnp.float32)
            for i in range(n):
                out_ref[0, :, pl.ds(at, lanes)] = level[i * own_bins : (i + 1) * own_bins] * scale
                at += lanes


def local(rng_count, chan_count, samples, phase_codes, block_pattern, steering):
    _, rx_count, pulses, gates = samples.shape
    chips = phase_codes.shape[1]
    _, beam_count, pair_count = steering.shape
    bins = pulses * chan_count
    own_bins = bins // rng_count
    blocks = BLOCKS
    chunks = len(blocks)
    vmem = pl.BlockSpec(memory_space=pltpu.VMEM)
    hbm = pl.BlockSpec(memory_space=pltpu.HBM)
    bf16 = jnp.bfloat16
    levels = pl.pallas_call(
        functools.partial(kernel, rng_count, chan_count, blocks),
        out_shape=[
            jax.ShapeDtypeStruct((rng_count, own_bins * n, LANES), bf16) for n in blocks
        ]
        + [jax.ShapeDtypeStruct((own_bins, LANES), jnp.float32)],
        in_specs=[hbm] * 5,
        out_specs=[hbm] * (chunks + 1),
        scratch_shapes=[
            pltpu.VMEM(phase_codes.shape, jnp.int32),
            pltpu.VMEM(block_pattern.shape[::-1], jnp.int32),
            pltpu.VMEM((2 * beam_count, pair_count), bf16),
            pltpu.VMEM((2, rx_count, pulses, gates + LANES), bf16),
            pltpu.VMEM((2 * bins, 2 * bins), bf16),
            pltpu.VMEM((2 * rx_count, beam_count, 2 * chips), jnp.float32),
            pltpu.VMEM((beam_count, rx_count * 2 * chips, 2 * LANES), bf16),
            pltpu.VMEM((2 * max(blocks) * pulses, rx_count * 2 * LANES), bf16),
            pltpu.SemaphoreType.DMA((5,)),
            pltpu.SemaphoreType.DMA((2,)),
            pltpu.SemaphoreType.DMA((chunks,)),
            pltpu.SemaphoreType.DMA((chunks,)),
            pltpu.SemaphoreType.DMA((chunks,)),
            pltpu.SemaphoreType.DMA((chunks,)),
            pltpu.VMEM((own_bins, LANES), jnp.float32),
            pltpu.SemaphoreType.DMA,
            *(pltpu.VMEM((beam_count, 2, pulses, n * LANES), bf16) for n in blocks),
            *(pltpu.VMEM((2, bins, n * LANES), bf16) for n in blocks),
            *(pltpu.VMEM((rng_count, own_bins * n, LANES), bf16) for n in blocks * 2),
        ],
        compiler_params=pltpu.CompilerParams(
            collective_id=0, has_side_effects=True, vmem_limit_bytes=VMEM_BYTES
        ),
        cost_estimate=pl.CostEstimate(
            flops=3 * 10**9, bytes_accessed=4 * 2**20, transcendentals=0
        ),
    )(
        samples,
        phase_codes,
        block_pattern.T,
        steering.reshape(2 * beam_count, pair_count),
        dft_table(bins),
    )
    return pl.pallas_call(
        functools.partial(finish, blocks),
        out_shape=jax.ShapeDtypeStruct((1, own_bins, gates * rng_count), jnp.float32),
        grid=(STEPS,),
        in_specs=[
            pl.BlockSpec((rng_count // STEPS, own_bins * n, LANES), lambda i: (i, 0, 0))
            for n in blocks
        ]
        + [pl.BlockSpec((own_bins, LANES), lambda i: (0, 0))],
        out_specs=pl.BlockSpec((1, own_bins, gates * rng_count // STEPS), lambda i: (0, 0, i)),
    )(*levels)


def solution(mesh):
    return jax.shard_map(
        functools.partial(local, mesh.shape["rng"], mesh.shape["chan"]),
        mesh=mesh,
        in_specs=(P(None, None, "chan", "rng"), P(), P(), P()),
        out_specs=P("chan", "rng", None),
        check_vma=False,
    )
```

```python
import functools
import math

import jax
import jax.numpy as jnp
import numpy as np
from jax import lax
from jax.experimental import pallas as pl
from jax.experimental.pallas import tpu as pltpu
from jax.sharding import PartitionSpec as P

PHASES = 16
LANES = 128
BLOCKS = (1, 1, 1, 1)
STEPS = 2
VMEM_BYTES = 64 * 2**20 - 2**17
MESH = pl.DeviceIdType.MESH


def dft_table(pulse_count):
    index = np.arange(pulse_count)
    angles = (np.outer(index, index) % pulse_count) * (2.0 * math.pi / pulse_count)
    cosine, sine = np.cos(angles), np.sin(angles)
    table = np.concatenate([cosine, sine], axis=1)
    return jnp.asarray(table, jnp.bfloat16)


def dot(left, right):
    return jnp.dot(left, right, preferred_element_type=jnp.float32)


def kernel(
    rng_count,
    chan_count,
    blocks,
    samples_ref,
    codes_hbm,
    pattern_hbm,
    steering_hbm,
    table_hbm,
    *refs,
):
    levels, scale_hbm = refs[: len(blocks)], refs[len(blocks)]
    (
        codes_ref,
        pattern_ref,
        steering_ref,
        extended,
        table,
        taps,
        filters,
        lines,
        load_sem,
        edge_sem,
        beam_send,
        beam_recv,
        power_send,
        power_recv,
        scale,
        scale_sem,
        *buffers,
    ) = refs[len(blocks) + 1 :]
    rng = lax.axis_index("rng")
    chan = lax.axis_index("chan")
    rx_count, pulses, gates = samples_ref.shape[1:]
    chips = codes_ref.shape[1]
    chunks = len(blocks)
    outgoing, gathered, power_out, power_in = (
        buffers[i * chunks : (i + 1) * chunks] for i in range(4)
    )
    starts = [sum(blocks[:i]) for i in range(chunks)]
    bins = table.shape[0]
    own_bins = bins // rng_count

    small = [
        pltpu.make_async_copy(codes_hbm, codes_ref, load_sem.at[0]),
        pltpu.make_async_copy(pattern_hbm, pattern_ref, load_sem.at[1]),
        pltpu.make_async_copy(steering_hbm, steering_ref, load_sem.at[2]),
    ]
    for copy in small:
        copy.start()
    load = pltpu.make_async_copy(
        samples_ref, extended.at[:, :, :, pl.ds(0, gates)], load_sem.at[3]
    )
    load.start()
    table_load = pltpu.make_async_copy(table_hbm, table, load_sem.at[4])
    table_load.start()

    barrier = pltpu.get_barrier_semaphore()

    @pl.loop(1, chan_count)
    def _(step):
        peer = lax.rem(chan + step, chan_count)
        pl.semaphore_signal(barrier, inc=1, device_id={"chan": peer}, device_id_type=MESH)

    @pl.loop(1, rng_count)
    def _(step):
        peer = lax.rem(rng + step, rng_count)
        pl.semaphore_signal(barrier, inc=1, device_id={"rng": peer}, device_id_type=MESH)

    for copy in small:
        copy.wait()
    block_count, tx_count = pattern_ref.shape
    spread = (
        lax.broadcasted_iota(jnp.int32, (block_count, chips), 1) // (chips // block_count)
        == lax.broadcasted_iota(jnp.int32, (block_count, chips), 0)
    ).astype(jnp.float32)
    active = lax.dot_general(
        pattern_ref[...].astype(jnp.float32),
        spread,
        (((0,), (0,)), ((), ())),
        preferred_element_type=jnp.float32,
    )
    phase = codes_ref[...].astype(jnp.float32) * (2.0 * math.pi / PHASES)
    code_re = (jnp.cos(phase) * active).astype(jnp.bfloat16)
    code_im = (jnp.sin(phase) * active).astype(jnp.bfloat16)
    reverse = (
        lax.rem(
            lax.broadcasted_iota(jnp.int32, (chips, 2 * chips), 0)
            + lax.broadcasted_iota(jnp.int32, (chips, 2 * chips), 1),
            2 * chips,
        )
        == 0
    ).astype(jnp.bfloat16)
    back_re = dot(code_re, reverse)
    back_im = dot(code_im, reverse)
    weights = steering_ref[...]
    beam_count = weights.shape[0] // 2
    row = lax.broadcasted_iota(jnp.int32, (rx_count * tx_count, 2 * chips), 0) // tx_count
    for rx in range(rx_count):
        wide_re = jnp.where(row == rx, jnp.concatenate([back_re] * rx_count, 0), 0.0)
        wide_im = jnp.where(row == rx, jnp.concatenate([back_im] * rx_count, 0), 0.0)
        by_re = dot(weights, wide_re.astype(jnp.bfloat16))
        by_im = dot(weights, wide_im.astype(jnp.bfloat16))
        taps[2 * rx] = by_re[:beam_count] + by_im[beam_count:]
        taps[2 * rx + 1] = by_re[beam_count:] - by_im[:beam_count]

    load.wait()

    def fill_lines(chunk):
        for part in range(2):
            for block in range(blocks[chunk]):
                at = (starts[chunk] + block) * LANES
                top = (part * blocks[chunk] + block) * pulses
                for rx in range(rx_count):
                    lines[pl.ds(top, pulses), pl.ds(rx * 2 * LANES, 2 * LANES)] = extended[
                        part, rx, :, pl.ds(at, 2 * LANES)
                    ]

    def fill_filter(beam):
        rows = taps[:, pl.ds(beam, 1), :]
        slanted = pltpu.roll(
            jnp.broadcast_to(rows, (2 * rx_count, 8, 2 * chips)), 0, 2, stride=1, stride_axis=1
        )
        for pair in range(chips // 16):
            first = pltpu.roll(slanted, 16 * pair, 2) if pair else slanted
            second = pltpu.roll(slanted, 16 * pair + 8, 2)
            both = jnp.concatenate([first, second], axis=1).astype(jnp.bfloat16)
            for rx in range(rx_count):
                for part in range(2):
                    for half in range(2):
                        filters[
                            beam,
                            pl.ds(rx * 2 * chips + half * chips + 16 * pair, 16),
                            pl.ds(part * LANES, LANES),
                        ] = both[2 * rx + part, :, half * LANES : (half + 1) * LANES]

    def form_beam(chunk, beam):
        rows = blocks[chunk] * pulses
        mixed = dot(lines[pl.ds(0, 2 * rows), :], filters[beam])
        real = mixed[:rows, :LANES] - mixed[rows:, LANES:]
        imag = mixed[rows:, :LANES] + mixed[:rows, LANES:]
        return real.astype(jnp.bfloat16), imag.astype(jnp.bfloat16)

    def put(chunk, target, values, top):
        for part in range(2):
            for block in range(blocks[chunk]):
                target[part, pl.ds(top, pulses), pl.ds(block * LANES, LANES)] = values[part][
                    block * pulses : (block + 1) * pulses
                ]

    mine = pl.ds(pl.multiple_of(chan * pulses, pulses), pulses)

    def beam_copy(chunk, beam):
        return pltpu.make_async_remote_copy(
            src_ref=outgoing[chunk].at[beam],
            dst_ref=gathered[chunk].at[:, mine, :],
            send_sem=beam_send.at[chunk],
            recv_sem=beam_recv.at[chunk],
            device_id={"chan": beam},
            device_id_type=MESH,
        )

    def partner(step):
        return lax.rem(chan // 2 + step % 4, chan_count // 2) * 2 + (chan + step // 4) % 2

    fill_lines(0)
    pl.semaphore_wait(barrier, rng_count + chan_count - 2)

    edge = pltpu.make_async_remote_copy(
        src_ref=extended.at[:, :, :, pl.ds(0, LANES)],
        dst_ref=extended.at[:, :, :, pl.ds(gates, LANES)],
        send_sem=edge_sem.at[0],
        recv_sem=edge_sem.at[1],
        device_id={"rng": lax.rem(rng + rng_count - 1, rng_count)},
        device_id_type=MESH,
    )
    edge.start()

    for chunk in range(chunks):
        if chunk:
            if chunk == chunks - 1:
                edge.wait()
                tail = extended[:, :, :, pl.ds(gates, LANES)]
                extended[:, :, :, pl.ds(gates, LANES)] = jnp.where(
                    rng == rng_count - 1, jnp.zeros_like(tail), tail
                )
            fill_lines(chunk)

        @pl.loop(1, chan_count)
        def _(step):
            beam = partner(step)
            if chunk == 0:
                fill_filter(beam)
            put(chunk, outgoing[chunk].at[beam], form_beam(chunk, beam), 0)
            beam_copy(chunk, beam).start()

        if chunk == 0:
            fill_filter(chan)
        put(chunk, gathered[chunk], form_beam(chunk, chan), pl.multiple_of(chan * pulses, pulses))

    def power_copy(chunk, peer):
        return pltpu.make_async_remote_copy(
            src_ref=power_out[chunk].at[peer],
            dst_ref=power_in[chunk].at[rng],
            send_sem=power_send.at[chunk],
            recv_sem=power_recv.at[chunk],
            device_id={"rng": peer},
            device_id_type=MESH,
        )

    table_load.wait()
    step_bins = 128
    for chunk in range(chunks):
        arrived = outgoing[chunk].at[pl.ds(0, chan_count - 1)]
        pltpu.make_async_copy(arrived, arrived, beam_recv.at[chunk]).wait()
        part_re, part_im = gathered[chunk][0], gathered[chunk][1]
        series = jnp.concatenate(
            [
                jnp.concatenate([part_re, part_im], axis=1),
                jnp.concatenate([part_im, -part_re], axis=1),
            ],
            axis=0,
        )
        width = blocks[chunk] * LANES
        for at in range(0, bins, step_bins):
            mixed = dot(table[pl.ds(at, step_bins), :], series)
            real, imag = mixed[:, :width], mixed[:, width:]
            real = real.astype(jnp.bfloat16).astype(jnp.float32)
            imag = imag.astype(jnp.bfloat16).astype(jnp.float32)
            power = (real * real + imag * imag).reshape(
                step_bins // own_bins, own_bins, blocks[chunk] * LANES
            )
            power = jnp.concatenate(
                [power[:, :, i * LANES : (i + 1) * LANES] for i in range(blocks[chunk])], axis=1
            )
            power_out[chunk][pl.ds(at // own_bins, step_bins // own_bins)] = power.astype(
                jnp.bfloat16
            )

        @pl.loop(1, rng_count, unroll=7)
        def _(step):
            power_copy(chunk, lax.rem(rng + step, rng_count)).start()

        power_in[chunk][rng] = power_out[chunk][rng]

    total = jnp.zeros((own_bins, LANES), jnp.float32)
    for chunk in range(chunks):
        arrived = power_in[chunk].at[pl.ds(0, rng_count - 1)]
        pltpu.make_async_copy(arrived, arrived, power_recv.at[chunk]).wait()
        pltpu.make_async_copy(power_in[chunk], levels[chunk], load_sem.at[chunk]).start()
        level = jnp.sum(power_in[chunk][...].astype(jnp.float32), axis=0)
        for i in range(blocks[chunk]):
            total = total + level[i * own_bins : (i + 1) * own_bins]
    average = jnp.sum(total, axis=1, keepdims=True) / float(rng_count * gates)
    scale[...] = jnp.broadcast_to(1.0 / (average + 1e-06), scale.shape)
    scale_store = pltpu.make_async_copy(scale, scale_hbm, scale_sem)
    scale_store.start()
    for chunk in range(chunks):
        sent = outgoing[chunk].at[pl.ds(0, chan_count - 1)]
        pltpu.make_async_copy(sent, sent, beam_send.at[chunk]).wait()
        sent = power_out[chunk].at[pl.ds(0, rng_count - 1)]
        pltpu.make_async_copy(sent, sent, power_send.at[chunk]).wait()
        pltpu.make_async_copy(power_in[chunk], levels[chunk], load_sem.at[chunk]).wait()
    scale_store.wait()


def finish(blocks, *refs):
    levels, scale_ref, out_ref = refs[:-2], refs[-2], refs[-1]
    sources, _, lanes = levels[0].shape
    own_bins = out_ref.shape[1]
    scale = scale_ref[...]
    at = 0
    for source in range(sources):
        for n, ref in zip(blocks, levels, strict=True):
            level = ref[source].astype(jnp.float32)
            for i in range(n):
                out_ref[0, :, pl.ds(at, lanes)] = level[i * own_bins : (i + 1) * own_bins] * scale
                at += lanes


def local(rng_count, chan_count, samples, phase_codes, block_pattern, steering):
    _, rx_count, pulses, gates = samples.shape
    chips = phase_codes.shape[1]
    _, beam_count, pair_count = steering.shape
    bins = pulses * chan_count
    own_bins = bins // rng_count
    blocks = BLOCKS
    chunks = len(blocks)
    vmem = pl.BlockSpec(memory_space=pltpu.VMEM)
    hbm = pl.BlockSpec(memory_space=pltpu.HBM)
    bf16 = jnp.bfloat16
    levels = pl.pallas_call(
        functools.partial(kernel, rng_count, chan_count, blocks),
        out_shape=[
            jax.ShapeDtypeStruct((rng_count, own_bins * n, LANES), bf16) for n in blocks
        ]
        + [jax.ShapeDtypeStruct((own_bins, LANES), jnp.float32)],
        in_specs=[hbm] * 5,
        out_specs=[hbm] * (chunks + 1),
        scratch_shapes=[
            pltpu.VMEM(phase_codes.shape, jnp.int32),
            pltpu.VMEM(block_pattern.shape[::-1], jnp.int32),
            pltpu.VMEM((2 * beam_count, pair_count), bf16),
            pltpu.VMEM((2, rx_count, pulses, gates + LANES), bf16),
            pltpu.VMEM((bins, 2 * bins), bf16),
            pltpu.VMEM((2 * rx_count, beam_count, 2 * chips), jnp.float32),
            pltpu.VMEM((beam_count, rx_count * 2 * chips, 2 * LANES), bf16),
            pltpu.VMEM((2 * max(blocks) * pulses, rx_count * 2 * LANES), bf16),
            pltpu.SemaphoreType.DMA((5,)),
            pltpu.SemaphoreType.DMA((2,)),
            pltpu.SemaphoreType.DMA((chunks,)),
            pltpu.SemaphoreType.DMA((chunks,)),
            pltpu.SemaphoreType.DMA((chunks,)),
            pltpu.SemaphoreType.DMA((chunks,)),
            pltpu.VMEM((own_bins, LANES), jnp.float32),
            pltpu.SemaphoreType.DMA,
            *(pltpu.VMEM((beam_count, 2, pulses, n * LANES), bf16) for n in blocks),
            *(pltpu.VMEM((2, bins, n * LANES), bf16) for n in blocks),
            *(pltpu.VMEM((rng_count, own_bins * n, LANES), bf16) for n in blocks * 2),
        ],
        compiler_params=pltpu.CompilerParams(
            collective_id=0, has_side_effects=True, vmem_limit_bytes=VMEM_BYTES
        ),
        cost_estimate=pl.CostEstimate(
            flops=3 * 10**9, bytes_accessed=4 * 2**20, transcendentals=0
        ),
    )(
        samples,
        phase_codes,
        block_pattern.T,
        steering.reshape(2 * beam_count, pair_count),
        dft_table(bins),
    )
    return pl.pallas_call(
        functools.partial(finish, blocks),
        out_shape=jax.ShapeDtypeStruct((1, own_bins, gates * rng_count), jnp.float32),
        grid=(STEPS,),
        in_specs=[
            pl.BlockSpec((rng_count // STEPS, own_bins * n, LANES), lambda i: (i, 0, 0))
            for n in blocks
        ]
        + [pl.BlockSpec((own_bins, LANES), lambda i: (0, 0))],
        out_specs=pl.BlockSpec((1, own_bins, gates * rng_count // STEPS), lambda i: (0, 0, i)),
    )(*levels)


def solution(mesh):
    return jax.shard_map(
        functools.partial(local, mesh.shape["rng"], mesh.shape["chan"]),
        mesh=mesh,
        in_specs=(P(None, None, "chan", "rng"), P(), P(), P()),
        out_specs=P("chan", "rng", None),
        check_vma=False,
    )
```
